32 devices in a mesh: dp: 4 (over y, x), fsdp: 8 (over z, core).
Axes of the slice: x: 2, y: 2, z: 4, core: 2. Of those that a mesh axis runs over, the one named last changes fastest.
Arguments:
- inputs: float32 [32, 197, 768], P(('dp', 'fsdp')), may hold values from -6 to 6
- cotangent: float32 [32, 197, 768], P(('dp', 'fsdp')), may hold values from -6 to 6
- counts: int32 [32], P(('dp', 'fsdp')), may hold values from 0 to 1, as said below
- qkv_weight: float32 [1769472], P(('dp', 'fsdp')), may hold values from -0.21875 to 0.21875
- proj_weight: float32 [589824], P(('dp', 'fsdp')), may hold values from -0.875 to 0.875
- up_weight: float32 [2359296], P(('dp', 'fsdp')), may hold values from -0.21875 to 0.21875
- down_weight: float32 [2359296], P(('dp', 'fsdp')), may hold values from -0.109375 to 0.109375
- vectors: float32 [9216], P(('dp', 'fsdp')), may hold values from -2 to 2
- qkv_moment: float32 [1769472], P(('dp', 'fsdp')), may hold values from -18 to 18
- proj_moment: float32 [589824], P(('dp', 'fsdp')), may hold values from -18 to 18
- up_moment: float32 [2359296], P(('dp', 'fsdp')), may hold values from -18 to 18
- down_moment: float32 [2359296], P(('dp', 'fsdp')), may hold values from -18 to 18
- vectors_moment: float32 [9216], P(('dp', 'fsdp')), may hold values from -18 to 18
- qkv_square: float32 [1769472], P(('dp', 'fsdp')), may hold values from 6.304 to 25.216
- proj_square: float32 [589824], P(('dp', 'fsdp')), may hold values from 1.13472 to 4.53888
- up_square: float32 [2359296], P(('dp', 'fsdp')), may hold values from 0.37824 to 1.51296
- down_square: float32 [2359296], P(('dp', 'fsdp')), may hold values from 1.13472 to 4.53888
- vectors_square: float32 [9216], P(('dp', 'fsdp')), may hold values from 3.152 to 12.608
Outputs:
- block_out: float32 [32, 197, 768], P(('dp', 'fsdp'))
- input_grad: float32 [32, 197, 768], P(('dp', 'fsdp'))
- qkv_grad: float32 [1769472], P(('dp', 'fsdp'))
- proj_grad: float32 [589824], P(('dp', 'fsdp'))
- up_grad: float32 [2359296], P(('dp', 'fsdp'))
- down_grad: float32 [2359296], P(('dp', 'fsdp'))
- vectors_grad: float32 [9216], P(('dp', 'fsdp'))
- qkv_updated: float32 [1769472], P(('dp', 'fsdp'))
- proj_updated: float32 [589824], P(('dp', 'fsdp'))
- up_updated: float32 [2359296], P(('dp', 'fsdp'))
- down_updated: float32 [2359296], P(('dp', 'fsdp'))
- vectors_change: float32 [9216], P(('dp', 'fsdp'))
- qkv_moment_new: float32 [1769472], P(('dp', 'fsdp'))
- proj_moment_new: float32 [589824], P(('dp', 'fsdp'))
- up_moment_new: float32 [2359296], P(('dp', 'fsdp'))
- down_moment_new: float32 [2359296], P(('dp', 'fsdp'))
- vectors_moment_new: float32 [9216], P(('dp', 'fsdp'))
- qkv_square_new: float32 [1769472], P(('dp', 'fsdp'))
- proj_square_new: float32 [589824], P(('dp', 'fsdp'))
- up_square_new: float32 [2359296], P(('dp', 'fsdp'))
- down_square_new: float32 [2359296], P(('dp', 'fsdp'))
- vectors_square_new: float32 [9216], P(('dp', 'fsdp'))
The draws below stay inside these ranges and needn't reach their ends.
Inputs may be any that keep to these rules, and one draw needn't show every extreme that they name: `counts`: the number of live image slots of each device, the live ones first; some device has all 1 live.
All inputs are finite; a program needn't handle non-finite values.
Results may differ from the reference program's by a relative error of at most 0.011.
Values may be sent and summed in bfloat16 or wider, within the bound.
A program may use at most 192 MiB of HBM per device.

```python
import math
import jax
import jax.numpy as jnp
from jax import lax

D = 768
HEADS = 12
HD = 64
FF = 3072
SLOTS = 1
IMG_TOK = 197
SLOT_ALL = 32
VEC = 9216
DEVICES = 32


def draw_counts(key, part):
    values = jax.random.randint(key, (DEVICES,), 0, SLOTS + 1)
    chosen = jax.random.randint(jax.random.fold_in(key, 11), (), 0, DEVICES)
    return values.at[chosen].set(SLOTS).astype(jnp.int32)


def draw_vectors(key, part):
    total = 8 * D + FF
    position = jnp.arange(total)
    is_gain = (position < D) | (position >= 5 * D) & (position < 6 * D)
    noise = jnp.clip(jax.random.normal(key, (total,), jnp.float32), -4.0, 4.0)
    return jnp.where(is_gain, 1.0 + 0.25 * noise, 0.5 * noise).astype(jnp.float32)


def block_scale(key, dims, cuts, low, high):
    def one(axis_at, parts):
        steps = jax.random.uniform(jax.random.fold_in(jax.random.fold_in(key, 6), axis_at), (parts,), jnp.float32, low / len(cuts), high / len(cuts))
        return jnp.repeat(jnp.exp(steps), dims[axis_at] // parts).reshape((-1,) + (1,) * (len(dims) - axis_at - 1))

    loudness = one(*cuts[0])
    for cut in cuts[1:]:
        loudness = loudness * one(*cut)
    return loudness


def normal_values(key, shape, scale, reach, cuts=(), kind=jnp.bfloat16):
    values = scale * jax.random.normal(key, shape, jnp.float32)
    if cuts:
        values = values * block_scale(key, shape, cuts, -0.22, 0.18)
    return jnp.clip(values, -reach, reach).astype(kind)


def setup_inputs(seed: int = 0) -> dict:
    key_of = jax.random.split(jax.random.key(seed), 19)
    inputs = normal_values(key_of[0], (SLOT_ALL, IMG_TOK, D), 1.0, 6.0, ((0, 32),), jnp.float32)
    cotangent = normal_values(key_of[1], (SLOT_ALL, IMG_TOK, D), 1.0, 6.0, ((0, 32),), jnp.float32)
    counts = draw_counts(jax.random.fold_in(key_of[18], 71), 0)
    qkv_weight = normal_values(key_of[3], (3 * D * D,), D ** -0.5, 0.21875, ((0, 32),), jnp.float32)
    proj_weight = normal_values(key_of[4], (D * D,), (D // 16) ** -0.5, 0.875, ((0, 32),), jnp.float32)
    up_weight = normal_values(key_of[5], (D * FF,), D ** -0.5, 0.21875, ((0, 32),), jnp.float32)
    down_weight = normal_values(key_of[6], (FF * D,), FF ** -0.5, 0.109375, ((0, 32),), jnp.float32)
    vectors = draw_vectors(jax.random.fold_in(key_of[18], 71), 0)
    qkv_moment = normal_values(key_of[8], (3 * D * D,), 3.0, 18.0, ((0, 32),), jnp.float32)
    proj_moment = normal_values(key_of[9], (D * D,), 3.0, 18.0, ((0, 32),), jnp.float32)
    up_moment = normal_values(key_of[10], (D * FF,), 3.0, 18.0, ((0, 32),), jnp.float32)
    down_moment = normal_values(key_of[11], (FF * D,), 3.0, 18.0, ((0, 32),), jnp.float32)
    vectors_moment = normal_values(key_of[12], (VEC,), 3.0, 18.0, ((0, 32),), jnp.float32)
    qkv_square = jnp.clip(jnp.exp(math.log(25.216) - 1.3862944 * jax.random.uniform(key_of[13], (3 * D * D,), jnp.float32) ** block_scale(key_of[13], (3 * D * D,), ((0, 32),), -0.2, 0.2)), 6.304, 25.216)
    proj_square = jnp.clip(jnp.exp(math.log(4.53888) - 1.3862944 * jax.random.uniform(key_of[14], (D * D,), jnp.float32) ** block_scale(key_of[14], (D * D,), ((0, 32),), -0.2, 0.2)), 1.13472, 4.53888)
    up_square = jnp.clip(jnp.exp(math.log(1.51296) - 1.3862944 * jax.random.uniform(key_of[15], (D * FF,), jnp.float32) ** block_scale(key_of[15], (D * FF,), ((0, 32),), -0.2, 0.2)), 0.37824, 1.51296)
    down_square = jnp.clip(jnp.exp(math.log(4.53888) - 1.3862944 * jax.random.uniform(key_of[16], (FF * D,), jnp.float32) ** block_scale(key_of[16], (FF * D,), ((0, 32),), -0.2, 0.2)), 1.13472, 4.53888)
    vectors_square = jnp.clip(jnp.exp(math.log(12.608) - 1.3862944 * jax.random.uniform(key_of[17], (VEC,), jnp.float32) ** block_scale(key_of[17], (VEC,), ((0, 32),), -0.2, 0.2)), 3.152, 12.608)
    return dict(inputs=inputs, cotangent=cotangent, counts=counts, qkv_weight=qkv_weight, proj_weight=proj_weight, up_weight=up_weight, down_weight=down_weight, vectors=vectors, qkv_moment=qkv_moment, proj_moment=proj_moment, up_moment=up_moment, down_moment=down_moment, vectors_moment=vectors_moment, qkv_square=qkv_square, proj_square=proj_square, up_square=up_square, down_square=down_square, vectors_square=vectors_square)


norm_eps = 1e-06
beta_first = 0.9
beta_second = 0.999
adam_eps = 1e-08
learn_rate = 0.02
weight_decay = 0.05
highest = lax.Precision.HIGHEST

def norm_stats(values):
    row_mean = lax.optimization_barrier(jnp.mean(values, axis=-1, keepdims=True))
    centered = values - row_mean
    inverse = lax.rsqrt(lax.optimization_barrier(jnp.mean(centered * centered, axis=-1, keepdims=True)) + norm_eps)
    return (centered * inverse, inverse)

def norm_back(grad_normed, normed, inverse):
    first_mean = lax.optimization_barrier(jnp.mean(grad_normed, axis=-1, keepdims=True))
    second_mean = lax.optimization_barrier(jnp.mean(grad_normed * normed, axis=-1, keepdims=True))
    return inverse * (grad_normed - first_mean - normed * second_mean)

def gelu_parts(pre_act):
    normal_cdf = 0.5 * (1.0 + lax.erf(pre_act * 0.7071067811865476))
    normal_pdf = jnp.exp(-0.5 * pre_act * pre_act) * 0.3989422804014327
    return (pre_act * normal_cdf, normal_cdf + pre_act * normal_pdf)

def split_vectors(vector_values):
    pieces = []
    for position in range(7):
        pieces.append(vector_values[position * D:(position + 1) * D])
    pieces.append(vector_values[7 * D:7 * D + FF])
    pieces.append(vector_values[7 * D + FF:8 * D + FF])
    return pieces

def mixed_dot(left_side, right_side):
    return jnp.dot(left_side, right_side, preferred_element_type=jnp.float32)

def wide_einsum(form, left_side, right_side):
    return jnp.einsum(form, left_side.astype(jnp.float32), right_side.astype(jnp.float32), precision=highest)

def block_pass(inputs, cotangent, live_mask, matrices):
    qkv_matrix, proj_matrix, up_matrix, down_matrix, vector_values = matrices
    gain_one, bias_one, bias_query, bias_value, bias_proj, gain_two, bias_two, bias_up, bias_down = split_vectors(vector_values)
    slot_count = inputs.shape[0]
    seq_len = inputs.shape[1]
    row_count = slot_count * seq_len
    head_shape = (slot_count, seq_len, HEADS, HD)
    score_scale = 1.0 / math.sqrt(HD)
    flat_rows = inputs.reshape(row_count, D)
    normed_one, inverse_one = norm_stats(flat_rows)
    act_one = (normed_one * gain_one + bias_one).astype(jnp.bfloat16)
    projected = mixed_dot(act_one, qkv_matrix)
    query_rows = (projected[:, :D] + bias_query).astype(jnp.bfloat16).reshape(head_shape)
    key_rows = projected[:, D:2 * D].astype(jnp.bfloat16).reshape(head_shape)
    value_rows = (projected[:, 2 * D:] + bias_value).astype(jnp.bfloat16).reshape(head_shape)
    scores = wide_einsum('sqhe,skhe->shqk', query_rows, key_rows) * score_scale
    row_max = lax.optimization_barrier(jnp.max(scores, axis=-1, keepdims=True))
    log_total = row_max + jnp.log(lax.optimization_barrier(jnp.sum(jnp.exp(scores - row_max), axis=-1, keepdims=True)))
    attn_probs = jnp.exp(scores - log_total)
    probs_low = attn_probs.astype(jnp.bfloat16)
    mixed_heads = wide_einsum('shqk,skhe->sqhe', probs_low, value_rows).astype(jnp.bfloat16).reshape(row_count, D)
    hidden = flat_rows + mixed_dot(mixed_heads, proj_matrix) + bias_proj
    normed_two, inverse_two = norm_stats(hidden)
    act_two = (normed_two * gain_two + bias_two).astype(jnp.bfloat16)
    pre_act = mixed_dot(act_two, up_matrix) + bias_up
    gelu_value, gelu_slope = gelu_parts(pre_act)
    gelu_low = gelu_value.astype(jnp.bfloat16)
    block_rows = hidden + mixed_dot(gelu_low, down_matrix) + bias_down
    block_out = block_rows.reshape(inputs.shape) * live_mask
    grad_rows = (cotangent * live_mask).reshape(row_count, D)
    grad_low = grad_rows.astype(jnp.bfloat16)
    down_grad = mixed_dot(gelu_low.T, grad_low)
    grad_pre = mixed_dot(grad_low, down_matrix.T) * gelu_slope
    grad_pre_low = grad_pre.astype(jnp.bfloat16)
    up_grad = mixed_dot(act_two.T, grad_pre_low)
    grad_act_two = mixed_dot(grad_pre_low, up_matrix.T)
    grad_hidden = grad_rows + norm_back(grad_act_two * gain_two, normed_two, inverse_two)
    grad_hidden_low = grad_hidden.astype(jnp.bfloat16)
    proj_grad = mixed_dot(mixed_heads.T, grad_hidden_low)
    grad_mixed = mixed_dot(grad_hidden_low, proj_matrix.T).astype(jnp.bfloat16).reshape(head_shape)
    grad_probs = wide_einsum('sqhe,skhe->shqk', grad_mixed, value_rows)
    grad_value = wide_einsum('shqk,sqhe->skhe', probs_low, grad_mixed).reshape(row_count, D)
    row_delta = lax.optimization_barrier(jnp.sum(attn_probs * grad_probs, axis=-1, keepdims=True))
    grad_scores = (attn_probs * (grad_probs - row_delta) * score_scale).astype(jnp.bfloat16)
    grad_query = wide_einsum('shqk,skhe->sqhe', grad_scores, key_rows).reshape(row_count, D)
    grad_key = wide_einsum('shqk,sqhe->skhe', grad_scores, query_rows).reshape(row_count, D)
    grad_proj_low = jnp.concatenate([grad_query, grad_key, grad_value], axis=1).astype(jnp.bfloat16)
    qkv_grad = mixed_dot(act_one.T, grad_proj_low)
    grad_act_one = mixed_dot(grad_proj_low, qkv_matrix.T)
    input_rows = grad_hidden + norm_back(grad_act_one * gain_one, normed_one, inverse_one)
    vectors_grad = jnp.concatenate([lax.optimization_barrier(jnp.sum(grad_act_one * normed_one, axis=0)), lax.optimization_barrier(jnp.sum(grad_act_one, axis=0)), lax.optimization_barrier(jnp.sum(grad_query, axis=0)), lax.optimization_barrier(jnp.sum(grad_value, axis=0)), lax.optimization_barrier(jnp.sum(grad_hidden, axis=0)), lax.optimization_barrier(jnp.sum(grad_act_two * normed_two, axis=0)), lax.optimization_barrier(jnp.sum(grad_act_two, axis=0)), lax.optimization_barrier(jnp.sum(grad_pre, axis=0)), lax.optimization_barrier(jnp.sum(grad_rows, axis=0))])
    return (block_out, input_rows.reshape(inputs.shape), qkv_grad, proj_grad, up_grad, down_grad, vectors_grad)

def adam_step(param, grad, moment, square):
    moment_new = beta_first * moment + (1.0 - beta_first) * grad
    square_new = beta_second * square + (1.0 - beta_second) * grad * grad
    moment_hat = moment_new / (1.0 - beta_first ** 3)
    square_hat = square_new / (1.0 - beta_second ** 3)
    change = -learn_rate * (moment_hat / (jnp.sqrt(square_hat) + adam_eps) + weight_decay * param)
    updated = param + change
    return (updated, moment_new, square_new, change)

def unpack(flats):
    return (flats[0].reshape(D, 3 * D), flats[1].reshape(D, D), flats[2].reshape(D, FF), flats[3].reshape(FF, D), flats[4].astype(jnp.float32))

def reference(inputs, cotangent, counts, qkv_weight, proj_weight, up_weight, down_weight, vectors, qkv_moment, proj_moment, up_moment, down_moment, vectors_moment, qkv_square, proj_square, up_square, down_square, vectors_square):
    params = (qkv_weight, proj_weight, up_weight, down_weight, vectors)
    matrices = unpack(tuple((param.astype(jnp.bfloat16) for param in params)))
    grouped = inputs.reshape(DEVICES, SLOTS, IMG_TOK, D)
    cot_grouped = cotangent.reshape(DEVICES, SLOTS, IMG_TOK, D)

    def device_step(running, device_item):
        device_inputs, device_cot, device_count = device_item
        live_mask = (jnp.arange(SLOTS, dtype=jnp.int32) < device_count).astype(jnp.float32).reshape(SLOTS, 1, 1)
        result = block_pass(device_inputs, device_cot, live_mask, matrices)
        running = tuple((summed + addend.reshape(-1) for summed, addend in zip(running, result[2:])))
        return (running, (result[0], result[1]))
    initial = tuple((jnp.zeros(param.shape, jnp.float32) for param in params))
    totals, (outs_all, grads_all) = lax.scan(device_step, initial, (grouped, cot_grouped, counts))
    block_out = outs_all.reshape(SLOT_ALL, IMG_TOK, D)
    input_grad = grads_all.reshape(SLOT_ALL, IMG_TOK, D)
    qkv_new = adam_step(qkv_weight, totals[0], qkv_moment, qkv_square)
    proj_new = adam_step(proj_weight, totals[1], proj_moment, proj_square)
    up_new = adam_step(up_weight, totals[2], up_moment, up_square)
    down_new = adam_step(down_weight, totals[3], down_moment, down_square)
    vectors_new = adam_step(vectors, totals[4], vectors_moment, vectors_square)
    return (block_out, input_grad, totals[0], totals[1], totals[2], totals[3], totals[4], qkv_new[0], proj_new[0], up_new[0], down_new[0], vectors_new[3], qkv_new[1], proj_new[1], up_new[1], down_new[1], vectors_new[1], qkv_new[2], proj_new[2], up_new[2], down_new[2], vectors_new[2])
```

```python
import functools
import math

import jax
import jax.numpy as jnp
from jax import lax
from jax.experimental import pallas as pl
from jax.experimental.pallas import tpu as pltpu
from jax.sharding import PartitionSpec as P

D = 768
HEADS = 12
HD = 64
FF = 3072


norm_eps = 1e-06
beta_first = 0.9
beta_second = 0.999
adam_eps = 1e-08
learn_rate = 0.02
weight_decay = 0.05


def norm_stats(values):
    row_mean = jnp.mean(values, axis=-1, keepdims=True)
    centered = values - row_mean
    inverse = lax.rsqrt(jnp.mean(centered * centered, axis=-1, keepdims=True) + norm_eps)
    return (centered * inverse, inverse)


def norm_back(grad_normed, normed, inverse):
    first_mean = jnp.mean(grad_normed, axis=-1, keepdims=True)
    second_mean = jnp.mean(grad_normed * normed, axis=-1, keepdims=True)
    return inverse * (grad_normed - first_mean - normed * second_mean)


def gelu_parts(pre_act):
    normal_cdf = 0.5 * (1.0 + lax.erf(pre_act * 0.7071067811865476))
    normal_pdf = jnp.exp(-0.5 * pre_act * pre_act) * 0.3989422804014327
    return (pre_act * normal_cdf, normal_cdf + pre_act * normal_pdf)


def split_vectors(vector_values):
    pieces = []
    for position in range(7):
        pieces.append(vector_values[position * D : (position + 1) * D])
    pieces.append(vector_values[7 * D : 7 * D + FF])
    pieces.append(vector_values[7 * D + FF : 8 * D + FF])
    return pieces


def mixed_dot(left_side, right_side):
    return jnp.dot(left_side, right_side, preferred_element_type=jnp.float32)


def low_einsum(form, left_side, right_side):
    return jnp.einsum(form, left_side, right_side, preferred_element_type=jnp.float32)


def outer_sum(left_side, right_side):
    return lax.dot_general(
        left_side, right_side, (((0,), (0,)), ((), ())), preferred_element_type=jnp.float32
    )


def block_rows_of(per):
    rows = -(-(12 * per + 1) // 8) * 8
    return rows if rows % 16 else rows + 8


def pack_shards(per, shards):
    qkv, proj, up, down, vectors = (shard.astype(jnp.bfloat16) for shard in shards)
    vec_row = jnp.pad(vectors, (0, D - vectors.shape[0])).reshape(1, D)
    parts = [qkv.reshape(per, 3 * D)[:, k * D : (k + 1) * D] for k in range(3)]
    parts.append(proj.reshape(per, D))
    parts += [up.reshape(per, FF)[:, k * D : (k + 1) * D] for k in range(4)]
    tail = block_rows_of(per) - 12 * per
    parts += [down.reshape(4 * per, D), jnp.pad(vec_row, ((0, tail - 1), (0, 0)))]
    return jnp.concatenate(parts, axis=0)


def unpack_matrices(per, blocks, vec_part):
    def piece(at):
        return blocks[:, at * per : (at + 1) * per].reshape(D, D)

    qkv_matrix = jnp.concatenate([piece(k) for k in range(3)], axis=1)
    up_matrix = jnp.concatenate([piece(4 + k) for k in range(4)], axis=1)
    down_matrix = blocks[:, 8 * per : 12 * per].reshape(FF, D)
    vector_values = blocks[:, 12 * per, :vec_part].reshape(-1).astype(jnp.float32)
    return (qkv_matrix, piece(3), up_matrix, down_matrix, vector_values)


def pack_grads(per, total, grads):
    low = [grad.astype(jnp.bfloat16) for grad in grads]
    vec_part = grads[4].shape[0] // total
    vec_cols = -(-vec_part // 128) * 128
    vec = jnp.pad(low[4].reshape(total, 1, vec_part), ((0, 0), (0, 15), (0, vec_cols - vec_part)))
    if per % 8 == 0:
        return [grad.reshape(total, -1, grad.shape[1]) for grad in low[:4]] + [vec]

    def piece(full, k):
        return full[:, k * D : (k + 1) * D].reshape(total, per, D)

    parts = [piece(low[0], k) for k in range(3)] + [piece(low[1], 0)]
    parts += [piece(low[2], k) for k in range(4)] + [low[3].reshape(total, 4 * per, D)]
    tail = block_rows_of(per) - 12 * per
    parts.append(jnp.pad(vec[:, :1], ((0, 0), (0, tail - 1), (0, D - vec_cols))))
    return [jnp.concatenate(parts, axis=1)]


def unpack_grads(per, pieces, vec_part):
    if len(pieces) > 1:
        return [piece.reshape(-1) for piece in pieces[:4]] + [pieces[4][0, :vec_part]]
    block = pieces[0]

    def side(first, count):
        return jnp.concatenate(
            [block[(first + k) * per : (first + k + 1) * per] for k in range(count)], axis=1
        ).reshape(-1)

    return (
        side(0, 3),
        block[3 * per : 4 * per].reshape(-1),
        side(4, 4),
        block[8 * per : 12 * per].reshape(-1),
        block[12 * per, :vec_part],
    )


def remote(src, dst, send, recv, where):
    return pltpu.make_async_remote_copy(
        src_ref=src, dst_ref=dst, send_sem=send, recv_sem=recv,
        device_id=where, device_id_type=pl.DeviceIdType.MESH,
    )


def greet_all(pair, dp_peer, z_peer, ndp, nz):
    barrier = pltpu.get_barrier_semaphore()

    def greet(where):
        pl.semaphore_signal(barrier, inc=1, device_id=where, device_id_type=pl.DeviceIdType.MESH)

    greet(pair)
    for j in range(1, ndp):
        greet(dp_peer(j))
    lax.fori_loop(1, nz, lambda j, carry: (greet(z_peer(j)), carry)[1], 0)
    pl.semaphore_wait(barrier, 1 + (ndp - 1) + (nz - 1))


def gather_kernel(ndp, nz, in_ref, out_ref, own_sem, zs, zr, ds, dr, ps, pr):
    d, f = lax.axis_index("dp"), lax.axis_index("fsdp")
    z, c = f // 2, f % 2
    pair = (d, z * 2 + 1 - c)

    def dp_peer(j):
        return (lax.rem(d + j, ndp), f)

    def z_peer(j):
        return (d, lax.rem(z + j, nz) * 2 + c)

    greet_all(pair, dp_peer, z_peer, ndp, nz)

    def from_z(t):
        return lax.rem(z - t + nz, nz)

    def from_dp(j):
        return lax.rem(d - j + ndp, ndp)

    def place(i, t, core):
        return out_ref.at[i, from_z(t), core]

    def z_send(t):
        return remote(in_ref, out_ref.at[d, z, c], zs.at[t - 1], zr.at[t - 1], z_peer(t))

    def z_arrival(t):
        return remote(in_ref, place(d, t, c), zs.at[t - 1], zr.at[t - 1], z_peer(t))

    def dp_send(t, j):
        return remote(
            place(d, t, c), place(d, t, c), ds.at[t, j - 1], dr.at[t, j - 1], dp_peer(j)
        )

    def dp_arrival(t, j):
        there = place(from_dp(j), t, c)
        return remote(there, there, ds.at[t, j - 1], dr.at[t, j - 1], dp_peer(j))

    def pair_send(t, j):
        here = place(from_dp(j), t, c)
        return remote(here, here, ps.at[t, j], pr.at[t, j], pair)

    def pair_arrival(t, j):
        there = place(from_dp(j), t, 1 - c)
        return remote(there, there, ps.at[t, j], pr.at[t, j], pair)

    lax.fori_loop(1, nz, lambda t, carry: (z_send(t).start(), carry)[1], 0)
    own = pltpu.make_async_copy(in_ref, out_ref.at[d, z, c], own_sem)
    own.start()
    own.wait()

    def forward(t):
        for j in range(1, ndp):
            dp_send(t, j).start()
        pair_send(t, 0).start()

    def spread(t):
        for j in range(1, ndp):
            dp_arrival(t, j).wait_recv()
            pair_send(t, j).start()

    def middle(t, carry):
        z_arrival(t).wait_recv()
        forward(t)
        spread(t - 1)
        return carry

    forward(0)
    lax.fori_loop(1, nz, middle, 0)
    spread(nz - 1)

    def close(t, carry):
        for j in range(ndp):
            pair_arrival(t, j).wait_recv()
            pair_send(t, j).wait_send()
        for j in range(1, ndp):
            dp_send(t, j).wait_send()
        return carry

    lax.fori_loop(0, nz, close, 0)
    lax.fori_loop(1, nz, lambda t, carry: (z_send(t).wait_send(), carry)[1], 0)


def gather_blocks(block, ndp, nf):
    rows = block.shape[0]
    nz = nf // 2
    dma = pltpu.SemaphoreType.DMA
    gathered = pl.pallas_call(
        functools.partial(gather_kernel, ndp, nz),
        out_shape=jax.ShapeDtypeStruct((ndp, nz, 2, rows, D), jnp.bfloat16),
        in_specs=[pl.BlockSpec(memory_space=pltpu.VMEM)],
        out_specs=pl.BlockSpec(memory_space=pl.ANY),
        scratch_shapes=[
            dma(()),
            dma((nz - 1,)),
            dma((nz - 1,)),
            dma((nz, ndp - 1)),
            dma((nz, ndp - 1)),
            dma((nz, ndp)),
            dma((nz, ndp)),
        ],
        compiler_params=pltpu.CompilerParams(
            collective_id=1, has_side_effects=True, vmem_limit_bytes=16 * 1024 * 1024
        ),
    )(block)
    return gathered.reshape(ndp * nf, rows, D)


def scatter_kernel(ndp, nz, count, *refs):
    g_refs, out_refs, pair_bufs, dp_bufs, z_bufs = (
        refs[k * count : (k + 1) * count] for k in range(5)
    )
    ps, pr, ds, dr, zs, zr = refs[5 * count :]
    pieces = range(count)
    d, f = lax.axis_index("dp"), lax.axis_index("fsdp")
    z, c = f // 2, f % 2
    oc = 1 - c
    pair = (d, z * 2 + oc)
    wide = jnp.float32

    def dp_peer(j):
        return (lax.rem(d + j, ndp), f)

    def z_peer(j):
        return (d, lax.rem(z + j, nz) * 2 + c)

    greet_all(pair, dp_peer, z_peer, ndp, nz)

    def target_z(t):
        return lax.rem(z + t + 1, nz)

    def pair_copy(t, i, k):
        return remote(
            g_refs[k].at[i, target_z(t), oc], pair_bufs[k].at[t, i],
            ps.at[t, i, k], pr.at[t, i, k], pair,
        )

    def dp_copy(t, j, k):
        where = dp_peer(j)
        return remote(
            pair_bufs[k].at[t, where[0]], dp_bufs[k].at[t, j - 1],
            ds.at[t, j - 1, k], dr.at[t, j - 1, k], where,
        )

    def z_copy(t, k):
        return remote(
            dp_bufs[k].at[t, 0], z_bufs[k].at[t], zs.at[t, k], zr.at[t, k], z_peer(t + 1)
        )

    def dp_of(j):
        return lax.rem(d + j, ndp)

    def open_pair(t):
        for j in range(1, ndp + 1):
            for k in pieces:
                pair_copy(t, dp_of(j), k).start()

    def chip_sum(t):
        for j in range(1, ndp + 1):
            i = dp_of(j)
            for k in pieces:
                pair_copy(t, i, k).wait_recv()
                mine = g_refs[k][i, target_z(t), c].astype(wide)
                pair_bufs[k][t, i] = (pair_bufs[k][t, i].astype(wide) + mine).astype(jnp.bfloat16)
                if j < ndp:
                    dp_copy(t, j, k).start()

    def dp_sum(t, k):
        running = pair_bufs[k][t, d].astype(wide)
        for j in range(1, ndp):
            dp_copy(t, j, k).wait_recv()
            running = running + dp_bufs[k][t, j - 1].astype(wide)
        return running

    def middle(t, carry):
        chip_sum(t)
        for k in pieces:
            dp_bufs[k][t - 1, 0] = dp_sum(t - 1, k).astype(jnp.bfloat16)
            z_copy(t - 1, k).start()
        return carry

    lax.fori_loop(0, nz, lambda t, carry: (open_pair(t), carry)[1], 0)
    chip_sum(0)
    lax.fori_loop(1, nz, middle, 0)
    for k in pieces:
        out_refs[k][...] = dp_sum(nz - 1, k)

    def last(t, carry):
        for k in pieces:
            z_copy(t, k).wait_recv()
            out_refs[k][...] += z_bufs[k][t].astype(wide)
        return carry

    lax.fori_loop(0, nz - 1, last, 0)

    def close(t, carry):
        for k in pieces:
            for i in range(ndp):
                pair_copy(t, i, k).wait_send()
            for j in range(1, ndp):
                dp_copy(t, j, k).wait_send()
        return carry

    lax.fori_loop(0, nz, close, 0)

    def close_z(t, carry):
        for k in pieces:
            z_copy(t, k).wait_send()
        return carry

    lax.fori_loop(0, nz - 1, close_z, 0)


def scatter_sum(pieces, ndp, nf):
    nz = nf // 2
    count = len(pieces)
    dma = pltpu.SemaphoreType.DMA
    shapes = [piece.shape[1:] for piece in pieces]
    whole_ref = pl.BlockSpec(memory_space=pltpu.VMEM)
    return pl.pallas_call(
        functools.partial(scatter_kernel, ndp, nz, count),
        out_shape=[jax.ShapeDtypeStruct(shape, jnp.float32) for shape in shapes],
        in_specs=[whole_ref] * count,
        out_specs=[whole_ref] * count,
        scratch_shapes=[pltpu.VMEM((nz, ndp) + shape, jnp.bfloat16) for shape in shapes]
        + [pltpu.VMEM((nz, ndp - 1) + shape, jnp.bfloat16) for shape in shapes]
        + [pltpu.VMEM((nz - 1,) + shape, jnp.bfloat16) for shape in shapes]
        + [
            dma((nz, ndp, count)),
            dma((nz, ndp, count)),
            dma((nz, ndp - 1, count)),
            dma((nz, ndp - 1, count)),
            dma((nz - 1, count)),
            dma((nz - 1, count)),
        ],
        compiler_params=pltpu.CompilerParams(
            collective_id=0, has_side_effects=True, vmem_limit_bytes=50 * 1024 * 1024
        ),
    )(*[piece.reshape((ndp, nz, 2) + shape) for piece, shape in zip(pieces, shapes)])


def adam_step(param, grad, moment, square):
    moment_new = beta_first * moment + (1.0 - beta_first) * grad
    square_new = beta_second * square + (1.0 - beta_second) * grad * grad
    moment_hat = moment_new / (1.0 - beta_first**3)
    square_hat = square_new / (1.0 - beta_second**3)
    change = -learn_rate * (moment_hat / (jnp.sqrt(square_hat) + adam_eps) + weight_decay * param)
    updated = param + change
    return (updated, moment_new, square_new, change)


def forward_pass(inputs, live_mask, matrices):
    qkv_matrix, proj_matrix, up_matrix, down_matrix, vector_values = matrices
    (
        gain_one,
        bias_one,
        bias_query,
        bias_value,
        bias_proj,
        gain_two,
        bias_two,
        bias_up,
        bias_down,
    ) = split_vectors(vector_values)
    slot_count = inputs.shape[0]
    seq_len = inputs.shape[1]
    row_count = slot_count * seq_len
    head_shape = (slot_count, seq_len, HEADS, HD)
    score_scale = 1.0 / math.sqrt(HD)
    flat_rows = inputs.reshape(row_count, D)
    normed_one, inverse_one = norm_stats(flat_rows)
    act_one = (normed_one * gain_one + bias_one).astype(jnp.bfloat16)
    projected = mixed_dot(act_one, qkv_matrix)
    query_rows = (projected[:, :D] + bias_query).astype(jnp.bfloat16).reshape(head_shape)
    key_rows = projected[:, D : 2 * D].astype(jnp.bfloat16).reshape(head_shape)
    value_rows = (projected[:, 2 * D :] + bias_value).astype(jnp.bfloat16).reshape(head_shape)
    scores = low_einsum("sqhe,skhe->shqk", query_rows, key_rows) * score_scale
    row_max = jnp.max(scores, axis=-1, keepdims=True)
    log_total = row_max + jnp.log(jnp.sum(jnp.exp(scores - row_max), axis=-1, keepdims=True))
    probs_low = jnp.exp(scores - log_total).astype(jnp.bfloat16)
    mixed_heads = (
        low_einsum("shqk,skhe->sqhe", probs_low, value_rows)
        .astype(jnp.bfloat16)
        .reshape(row_count, D)
    )
    hidden = flat_rows + mixed_dot(mixed_heads, proj_matrix) + bias_proj
    normed_two, inverse_two = norm_stats(hidden)
    act_two = (normed_two * gain_two + bias_two).astype(jnp.bfloat16)
    pre_act = mixed_dot(act_two, up_matrix) + bias_up
    gelu_value, gelu_slope = gelu_parts(pre_act)
    gelu_low = gelu_value.astype(jnp.bfloat16)
    block_rows = hidden + mixed_dot(gelu_low, down_matrix) + bias_down
    block_out = block_rows.reshape(inputs.shape) * live_mask
    saved = (
        normed_one,
        inverse_one,
        act_one,
        query_rows,
        key_rows,
        value_rows,
        log_total,
        mixed_heads,
        normed_two,
        inverse_two,
        act_two,
        gelu_low,
        gelu_slope,
    )
    return (block_out, saved)


def mlp_backward(saved, grad_rows, matrices):
    normed_two, inverse_two, gelu_slope = (saved[8], saved[9], saved[12])
    up_matrix, down_matrix, vector_values = (matrices[2], matrices[3], matrices[4])
    gain_two = split_vectors(vector_values)[5]
    grad_low = grad_rows.astype(jnp.bfloat16)
    grad_pre = mixed_dot(grad_low, down_matrix.T) * gelu_slope
    grad_pre_low = grad_pre.astype(jnp.bfloat16)
    grad_act_two = mixed_dot(grad_pre_low, up_matrix.T)
    grad_hidden = grad_rows + norm_back(grad_act_two * gain_two, normed_two, inverse_two)
    mlp_sums = [
        jnp.sum(grad_act_two * normed_two, axis=0),
        jnp.sum(grad_act_two, axis=0),
        jnp.sum(grad_pre, axis=0),
        jnp.sum(grad_rows, axis=0),
    ]
    return (grad_hidden, grad_low, grad_pre_low, mlp_sums)


def attn_backward(saved, grad_hidden, matrices):
    normed_one, inverse_one, query_rows, key_rows, value_rows, log_total = (
        saved[0],
        saved[1],
        saved[3],
        saved[4],
        saved[5],
        saved[6],
    )
    qkv_matrix, proj_matrix, vector_values = (matrices[0], matrices[1], matrices[4])
    gain_one = split_vectors(vector_values)[0]
    head_shape = query_rows.shape
    row_count = head_shape[0] * head_shape[1]
    score_scale = 1.0 / math.sqrt(HD)
    grad_hidden_low = grad_hidden.astype(jnp.bfloat16)
    grad_mixed = mixed_dot(grad_hidden_low, proj_matrix.T).astype(jnp.bfloat16).reshape(head_shape)
    scores = low_einsum("sqhe,skhe->shqk", query_rows, key_rows) * score_scale
    attn_probs = jnp.exp(scores - log_total)
    probs_low = attn_probs.astype(jnp.bfloat16)
    grad_probs = low_einsum("sqhe,skhe->shqk", grad_mixed, value_rows)
    grad_value = low_einsum("shqk,sqhe->skhe", probs_low, grad_mixed).reshape(row_count, D)
    row_delta = jnp.sum(attn_probs * grad_probs, axis=-1, keepdims=True)
    grad_scores = (attn_probs * (grad_probs - row_delta) * score_scale).astype(jnp.bfloat16)
    grad_query = low_einsum("shqk,skhe->sqhe", grad_scores, key_rows).reshape(row_count, D)
    grad_key = low_einsum("shqk,sqhe->skhe", grad_scores, query_rows).reshape(row_count, D)
    grad_proj_low = jnp.concatenate([grad_query, grad_key, grad_value], axis=1).astype(jnp.bfloat16)
    grad_act_one = mixed_dot(grad_proj_low, qkv_matrix.T)
    input_rows = grad_hidden + norm_back(grad_act_one * gain_one, normed_one, inverse_one)
    attn_sums = [
        jnp.sum(grad_act_one * normed_one, axis=0),
        jnp.sum(grad_act_one, axis=0),
        jnp.sum(grad_query, axis=0),
        jnp.sum(grad_value, axis=0),
        jnp.sum(grad_hidden, axis=0),
    ]
    return (input_rows, grad_proj_low, grad_hidden_low, attn_sums)


def body(
    ndp,
    nf,
    inputs,
    cotangent,
    counts,
    qkv_weight,
    proj_weight,
    up_weight,
    down_weight,
    vectors,
    qkv_moment,
    proj_moment,
    up_moment,
    down_moment,
    vectors_moment,
    qkv_square,
    proj_square,
    up_square,
    down_square,
    vectors_square,
):
    shards = (qkv_weight, proj_weight, up_weight, down_weight, vectors)
    total = ndp * nf
    per = D // total
    vec_part = vectors.shape[0]
    gathered = gather_blocks(pack_shards(per, shards), ndp, nf)
    matrices = unpack_matrices(per, gathered, vec_part)
    slot_count = inputs.shape[0]
    live_mask = (
        (jnp.arange(slot_count, dtype=jnp.int32) < counts[0])
        .astype(jnp.float32)
        .reshape(slot_count, 1, 1)
    )
    block_out, saved = forward_pass(inputs, live_mask, matrices)
    act_one, mixed_heads, act_two, gelu_low = (saved[2], saved[7], saved[10], saved[11])
    grad_rows = (cotangent * live_mask).reshape(-1, D)
    grad_hidden, grad_low, grad_pre_low, mlp_sums = mlp_backward(saved, grad_rows, matrices)
    down_full = outer_sum(gelu_low, grad_low)
    up_full = outer_sum(act_two, grad_pre_low)
    input_rows, grad_proj_low, grad_hidden_low, attn_sums = attn_backward(
        saved, grad_hidden, matrices
    )
    vectors_grad = jnp.concatenate(attn_sums + mlp_sums)
    qkv_full = outer_sum(act_one, grad_proj_low)
    proj_full = outer_sum(mixed_heads, grad_hidden_low)
    packed = pack_grads(per, total, (qkv_full, proj_full, up_full, down_full, vectors_grad))
    summed = scatter_sum(packed, ndp, nf)
    qkv_total, proj_total, up_total, down_total, vectors_total = unpack_grads(per, summed, vec_part)
    input_grad = input_rows.reshape(inputs.shape)
    qkv_new = adam_step(qkv_weight, qkv_total, qkv_moment, qkv_square)
    proj_new = adam_step(proj_weight, proj_total, proj_moment, proj_square)
    up_new = adam_step(up_weight, up_total, up_moment, up_square)
    down_new = adam_step(down_weight, down_total, down_moment, down_square)
    vectors_new = adam_step(vectors, vectors_total, vectors_moment, vectors_square)
    return (
        block_out,
        input_grad,
        qkv_total,
        proj_total,
        up_total,
        down_total,
        vectors_total,
        qkv_new[0],
        proj_new[0],
        up_new[0],
        down_new[0],
        vectors_new[3],
        qkv_new[1],
        proj_new[1],
        up_new[1],
        down_new[1],
        vectors_new[1],
        qkv_new[2],
        proj_new[2],
        up_new[2],
        down_new[2],
        vectors_new[2],
    )


def solution(mesh):
    placed = (
        P(("dp", "fsdp"), None, None),
        P(("dp", "fsdp"), None, None),
        P(("dp", "fsdp")),
        P(("dp", "fsdp")),
        P(("dp", "fsdp")),
        P(("dp", "fsdp")),
        P(("dp", "fsdp")),
        P(("dp", "fsdp")),
        P(("dp", "fsdp")),
        P(("dp", "fsdp")),
        P(("dp", "fsdp")),
        P(("dp", "fsdp")),
        P(("dp", "fsdp")),
        P(("dp", "fsdp")),
        P(("dp", "fsdp")),
        P(("dp", "fsdp")),
        P(("dp", "fsdp")),
        P(("dp", "fsdp")),
    )
    return jax.shard_map(
        functools.partial(body, mesh.shape["dp"], mesh.shape["fsdp"]),
        mesh=mesh,
        in_specs=placed,
        out_specs=(
            P(("dp", "fsdp"), None, None),
            P(("dp", "fsdp"), None, None),
            P(("dp", "fsdp")),
            P(("dp", "fsdp")),
            P(("dp", "fsdp")),
            P(("dp", "fsdp")),
            P(("dp", "fsdp")),
            P(("dp", "fsdp")),
            P(("dp", "fsdp")),
            P(("dp", "fsdp")),
            P(("dp", "fsdp")),
            P(("dp", "fsdp")),
            P(("dp", "fsdp")),
            P(("dp", "fsdp")),
            P(("dp", "fsdp")),
            P(("dp", "fsdp")),
            P(("dp", "fsdp")),
            P(("dp", "fsdp")),
            P(("dp", "fsdp")),
            P(("dp", "fsdp")),
            P(("dp", "fsdp")),
            P(("dp", "fsdp")),
        ),
        check_vma=False,
    )
```
